256 devices in a mesh: dp: 8 (over y, z_hi), dap: 32 (over z_lo, x, core).
Axes of the slice: x: 4, y: 4, z: 8 (z_hi: 2, z_lo: 4; z = z_hi * 4 + z_lo), core: 2. Of those that a mesh axis runs over, the one named last changes fastest.
Arguments:
- pair_act: bfloat16 [8, 256, 256, 128], P('dp', 'dap'), may hold values from -6 to 6
- cotangent: bfloat16 [8, 256, 256, 128], P('dp', 'dap'), may hold values from -6 to 6
- residue_mask: int32 [8, 256], P('dp'), may hold values 0 or 1
- in_gain: float32 [128], replicated, may hold values from 0.25 to 1.75
- out_gain: float32 [128], replicated, may hold values from 0.25 to 1.75
- in_weight: bfloat16 [128, 640], replicated, may hold values from -0.5 to 0.5
- out_weight: bfloat16 [128, 128], replicated, may hold values from -0.5 to 0.5
Outputs:
- pair_grad: bfloat16 [8, 256, 256, 128], P('dp', 'dap')
- in_weight_grad: float32 [128, 640], replicated
- out_weight_grad: float32 [128, 128], replicated
The draws below stay inside these ranges and needn't reach their ends.
Inputs may be any that keep to these rules, and one draw needn't show every extreme that they name: `residue_mask`: 1 marks a real residue, 0 padding.
All inputs are finite; a program needn't handle non-finite values. No bound on the sum of `residue_mask` on one device may be relied on, other than what follows from the above.
Results may differ from the reference program's by a relative error of at most 0.014.
Values may be sent and summed in bfloat16 or wider, within the bound.
A program may use at most 192 MiB of HBM per device.

```python
import math
import jax
import jax.numpy as jnp
from jax import lax

CH = 128
HID = 128
RES = 256
CROPS = 8


def place_ends(array, stream_key, low, high):
    extent = array.shape
    index_at = [jax.random.randint(jax.random.fold_in(stream_key, axis), (), 0, extent[axis]) for axis in range(len(extent))]
    array = array.at[tuple(index_at)].set(low)
    longest = extent.index(max(extent))
    index_at[longest] = (index_at[longest] + 1) % extent[longest]
    return array.at[tuple(index_at)].set(high)


def level_of(own_key, extent, cuts, least, largest):
    def one(position, parts):
        heights = jax.random.uniform(jax.random.fold_in(jax.random.fold_in(own_key, 6), position), (parts,), jnp.float32, least / len(cuts), largest / len(cuts))
        return jnp.repeat(jnp.exp(heights), extent[position] // parts).reshape((-1,) + (1,) * (len(extent) - position - 1))

    gain = one(*cuts[0])
    for cut in cuts[1:]:
        gain = gain * one(*cut)
    return gain


def centred(own_key, dims, scale, limit, cuts=(), kind=jnp.bfloat16):
    gain = level_of(own_key, dims, cuts, -0.22, 0.18) if cuts else 1.0
    entries = jax.random.normal(own_key, dims, jnp.float32) * scale * gain
    return jnp.minimum(jnp.maximum(entries, -limit), limit).astype(kind)


def setup_inputs(seed: int = 0) -> dict:
    streams_of = jax.random.split(jax.random.key(seed), 8)
    return {
        "pair_act": centred(streams_of[0], (CROPS, RES, RES, CH), 1.0, 6.0, ((0, 8), (1, 32))),
        "cotangent": centred(streams_of[1], (CROPS, RES, RES, CH), 1.0, 6.0, ((0, 8), (1, 32))),
        "residue_mask": place_ends((jax.random.randint(streams_of[2], (CROPS, RES), 0, 8) < 7).astype(jnp.int32), jax.random.fold_in(streams_of[2], 1), 0, 1),
        "in_gain": jnp.clip(1.0 + 0.15 * jax.random.normal(streams_of[3], (CH,), jnp.float32), 0.25, 1.75),
        "out_gain": jnp.clip(1.0 + 0.15 * jax.random.normal(streams_of[4], (HID,), jnp.float32), 0.25, 1.75),
        "in_weight": centred(streams_of[5], (CH, 5 * HID), CH ** -0.5, 0.5),
        "out_weight": centred(streams_of[6], (HID, CH), HID ** -0.5, 0.5),
    }


def layer_norm(values, norm_gain):
    centre = values - lax.optimization_barrier(jnp.mean(values, axis=-1, keepdims=True))
    spread = lax.optimization_barrier(jnp.mean(centre * centre, axis=-1, keepdims=True))
    return centre * lax.rsqrt(spread + 1e-05) * norm_gain

def crop_backward(pair_one, cotan_one, mask_one, in_gain, out_gain, in_weight, out_weight):
    mask_real = mask_one.astype(jnp.float32)
    mask_cells = (mask_real[:, None] * mask_real[None, :])[:, :, None]
    pair_real = pair_one.astype(jnp.float32)
    normed_real, pull_in = jax.vjp(lambda values: layer_norm(values, in_gain), pair_real)
    normed = normed_real.astype(jnp.bfloat16)
    proj = jnp.dot(normed.reshape(-1, CH), in_weight, preferred_element_type=jnp.float32).reshape(RES, RES, 5 * HID)
    proj_a, gate_a, proj_b, gate_b, gate_o = jnp.split(proj, 5, axis=-1)
    sig_a = jax.nn.sigmoid(gate_a)
    sig_b = jax.nn.sigmoid(gate_b)
    sig_o = jax.nn.sigmoid(gate_o)
    left = (sig_a * proj_a * mask_cells).astype(jnp.bfloat16)
    right = (sig_b * proj_b * mask_cells).astype(jnp.bfloat16)
    tri = jnp.einsum('ikc,jkc->ijc', left.astype(jnp.float32), right.astype(jnp.float32))
    tri_real, pull_out = jax.vjp(lambda values: layer_norm(values, out_gain), tri)
    tri_normed = tri_real.astype(jnp.bfloat16)
    projected = jnp.dot(tri_normed.reshape(-1, HID), out_weight, preferred_element_type=jnp.float32).reshape(RES, RES, CH)
    cotan_real = cotan_one.astype(jnp.float32)
    gated_grad = (cotan_real * sig_o).astype(jnp.bfloat16)
    grad_gate_o = cotan_real * projected * sig_o * (1.0 - sig_o)
    grad_normed_tri = jnp.dot(gated_grad.reshape(-1, CH), out_weight.T, preferred_element_type=jnp.float32).reshape(RES, RES, HID)
    grad_tri = pull_out(grad_normed_tri)[0].astype(jnp.bfloat16)
    grad_left = jnp.einsum('ijc,jkc->ikc', grad_tri.astype(jnp.float32), right.astype(jnp.float32))
    grad_right = jnp.einsum('ijc,ikc->jkc', grad_tri.astype(jnp.float32), left.astype(jnp.float32))
    pieces = [grad_left * sig_a * mask_cells, grad_left * proj_a * mask_cells * sig_a * (1.0 - sig_a), grad_right * sig_b * mask_cells, grad_right * proj_b * mask_cells * sig_b * (1.0 - sig_b), grad_gate_o]
    grad_proj = jnp.concatenate(pieces, axis=-1).astype(jnp.bfloat16)
    in_part = jnp.dot(normed.reshape(-1, CH).T, grad_proj.reshape(-1, 5 * HID), preferred_element_type=jnp.float32)
    out_part = jnp.dot(tri_normed.reshape(-1, HID).T, gated_grad.reshape(-1, CH), preferred_element_type=jnp.float32)
    grad_normed = jnp.dot(grad_proj.reshape(-1, 5 * HID), in_weight.T, preferred_element_type=jnp.float32).reshape(RES, RES, CH)
    pair_grad = pull_in(grad_normed)[0].astype(jnp.bfloat16)
    return (pair_grad, in_part, out_part)

def reference(pair_act, cotangent, residue_mask, in_gain, out_gain, in_weight, out_weight):

    def one_crop(inputs):
        return crop_backward(inputs[0], inputs[1], inputs[2], in_gain, out_gain, in_weight, out_weight)
    pair_grad, in_parts, out_parts = lax.map(one_crop, (pair_act, cotangent, residue_mask))
    factor = 1.0 / math.sqrt(CROPS * RES * RES)
    return (pair_grad, lax.optimization_barrier(jnp.sum(in_parts, axis=0)) * factor, lax.optimization_barrier(jnp.sum(out_parts, axis=0)) * factor)
```

```python
import functools
import math

import jax
import jax.numpy as jnp
from jax import lax
from jax.experimental import pallas as pl
from jax.experimental.pallas import tpu as pltpu
from jax.sharding import PartitionSpec as P

MESH = pl.DeviceIdType.MESH
F32 = jnp.float32
BF16 = jnp.bfloat16
LANES = 128
NT = (((1,), (1,)), ((), ()))


def dot(a, b):
    return jnp.dot(a, b, preferred_element_type=F32)


def dot_nt(a, b):
    return lax.dot_general(a, b, NT, preferred_element_type=F32)


def sigmoid(x):
    return 0.5 * jnp.tanh(0.5 * x) + 0.5


def kernel(
    dims,
    pair_ref, cot_ref, mask_ref, gin_ref, gout_ref, win_ref, wout_ref,
    out_ref, inw_ref, outw_ref,
    send, recv, stage_a, stage_b, left_m, right_m, grad_m, prod,
    xhat, rstd_in, normed, fac_a, fac_ga, fac_b, fac_gb, fac_o, gated, gnt, tri_n, gproj,
    part, recv1, sum1, recv2, sum2, recv3,
    send_sem, recv_sem, wsend_sem, wrecv_sem,
):
    n_dp, n_dap, rows, res, ch = dims
    per = ch // n_dap
    blk = per * rows
    halves = res // LANES
    me = lax.axis_index("dap")
    my_dp = lax.axis_index("dp")

    barrier = pltpu.get_barrier_semaphore()

    def greet(s, carry):
        pl.semaphore_signal(
            barrier, inc=1, device_id={"dap": lax.rem(me + s, n_dap)}, device_id_type=MESH
        )
        return carry

    lax.fori_loop(1, n_dap, greet, 0)

    def greet_dp(s, carry):
        pl.semaphore_signal(
            barrier, inc=1, device_id={"dp": lax.rem(my_dp + s, n_dp)}, device_id_type=MESH
        )
        return carry

    lax.fori_loop(1, n_dp, greet_dp, 0)

    def scatter(index, fill):
        def body(s, carry):
            peer = lax.rem(me + s, n_dap)
            fill(peer)
            pltpu.make_async_remote_copy(
                src_ref=send.at[index, peer],
                dst_ref=recv.at[index, me],
                send_sem=send_sem.at[index],
                recv_sem=recv_sem.at[index],
                device_id={"dap": peer},
                device_id_type=MESH,
            ).start()
            return carry

        lax.fori_loop(1, n_dap, body, 0)
        fill(me)
        pltpu.make_async_copy(
            send.at[index, me], recv.at[index, me], recv_sem.at[index]
        ).start()

    def arrived(index):
        pltpu.make_async_copy(recv.at[index], recv.at[index], recv_sem.at[index]).wait()

    def from_stage(index, stage):
        def fill(peer):
            at = pl.multiple_of(peer * blk, blk)
            block = [stage[pl.ds(at + h * rows * ch, blk), :] for h in range(halves)]
            send[index, peer] = jnp.concatenate(block, axis=1).astype(BF16)

        return fill

    def from_prod(index, base):
        def fill(peer):
            at = pl.multiple_of(peer * rows, rows)
            block = [prod[base + c, pl.ds(at, rows), :] for c in range(per)]
            send[index, peer] = jnp.concatenate(block, axis=0).astype(BF16)

        return fill

    def to_stage(index, stage):
        def body(d, carry):
            at = pl.multiple_of(d * blk, blk)
            block = recv[index, d].astype(F32)
            for h in range(halves):
                stage[pl.ds(at + h * rows * ch, blk), :] = block[:, h * LANES:(h + 1) * LANES]
            return carry

        lax.fori_loop(0, n_dap, body, 0, unroll=4)

    def to_matrices(index, mats):
        def body(pair, carry):
            low = recv[index, 2 * pair].astype(F32)
            high = recv[index, 2 * pair + 1].astype(F32)
            at = pl.multiple_of(pair * 2 * rows, 2 * rows)
            for c in range(per):
                cut = slice(c * rows, (c + 1) * rows)
                both = jnp.concatenate([low[cut], high[cut]], axis=0)
                mats[c, pl.ds(at, 2 * rows), :] = both.astype(BF16)
            return carry

        lax.fori_loop(0, n_dap // 2, body, 0, unroll=2)

    def put(stage, i, values):
        for h in range(halves):
            at = pl.ds(h * rows * ch + i, ch, stride=rows)
            stage[at, :] = values[:, h * LANES:(h + 1) * LANES]

    def take(stage, i):
        return jnp.concatenate(
            [stage[pl.ds(h * rows * ch + i, ch, stride=rows), :] for h in range(halves)], axis=1
        )

    ident = (
        lax.broadcasted_iota(jnp.int32, (res, res), 0)
        == lax.broadcasted_iota(jnp.int32, (res, res), 1)
    ).astype(F32).astype(BF16)
    ident_ch = ident[:ch, :ch]

    def column(row):
        square = jnp.broadcast_to(row, (ch, ch)).T
        return jnp.concatenate([square] * (res // ch), axis=1)

    gin = column(gin_ref[...])
    gout = column(gout_ref[...])
    win = win_ref[...]
    win_t = win.astype(F32).T.astype(BF16)
    wout = wout_ref[...]
    wout_t = wout.astype(F32).T.astype(BF16)
    mask_real = mask_ref[...].astype(F32)
    lane = lax.broadcasted_iota(jnp.int32, (1, res), 1)

    def mask_cells(i):
        own = jnp.where(lane == me * rows + i, mask_real, 0.0)
        return jnp.sum(own, axis=1, keepdims=True) * mask_real

    def norm(values):
        centre = values - jnp.mean(values, axis=0, keepdims=True)
        spread = jnp.mean(centre * centre, axis=0, keepdims=True)
        scale = lax.rsqrt(spread + 1e-05)
        return centre * scale, scale

    def norm_back(grad, hat, scale):
        first = jnp.mean(grad, axis=0, keepdims=True)
        second = jnp.mean(grad * hat, axis=0, keepdims=True)
        return scale * (grad - first - hat * second)

    def lanes(i):
        return pl.ds(pl.multiple_of(i * res, res), res)

    def gate_side(i, offset, stage, fac, fac_gate):
        both = dot(win_t[offset:offset + 2 * ch], normed[:, lanes(i)])
        value, gate = both[:ch], both[ch:]
        sig = sigmoid(gate)
        masked = sig * mask_cells(i)
        side = masked * value
        fac[i] = masked
        fac_gate[i] = side * (1.0 - sig)
        put(stage, i, side)

    for i in range(rows):
        pair_t = dot_nt(ident_ch, pair_ref[i])
        hat, scale = norm(pair_t)
        xhat[i] = hat
        rstd_in[i] = scale
        normed[:, i * res:(i + 1) * res] = (hat * gin).astype(BF16)
        gate_side(i, 2 * ch, stage_b, fac_b, fac_gb)

    pl.semaphore_wait(barrier, n_dap + n_dp - 2)
    scatter(0, from_stage(0, stage_b))
    for i in range(rows):
        gate_side(i, 0, stage_a, fac_a, fac_ga)
    scatter(1, from_stage(1, stage_a))

    for i in range(rows):
        gate_o = dot(win_t[4 * ch:], normed[:, i * res:(i + 1) * res])
        sig = sigmoid(gate_o)
        cot_t = dot_nt(ident_ch, cot_ref[i])
        gated_real = cot_t * sig
        fac_o[i] = gated_real * (1.0 - sig)
        gated_grad = gated_real.astype(BF16)
        gated[:, i * res:(i + 1) * res] = gated_grad
        gnt[i] = dot(wout, gated_grad) * gout

    arrived(0)
    to_matrices(0, right_m)
    arrived(1)
    to_matrices(1, left_m)
    for c in range(per):
        prod[c] = dot_nt(left_m[c], right_m[c])
    scatter(2, from_prod(2, 0))

    arrived(2)
    to_stage(2, stage_a)
    for i in range(rows):
        hat, scale = norm(take(stage_a, i))
        tri_n[:, i * res:(i + 1) * res] = (hat * gout).astype(BF16)
        put(stage_b, i, norm_back(gnt[i], hat, scale))
    scatter(3, from_stage(3, stage_b))
    for i in range(rows):
        projected = dot(wout_t, tri_n[:, i * res:(i + 1) * res])
        gproj[4 * ch:, i * res:(i + 1) * res] = (projected * fac_o[i]).astype(BF16)
    out_part = dot_nt(tri_n[...], gated[...])

    arrived(3)
    to_matrices(3, grad_m)
    for c in range(per):
        flip = grad_m[c].astype(F32).T.astype(BF16)
        prod[c] = dot(flip, left_m[c])
    scatter(4, from_prod(4, 0))
    for c in range(per):
        prod[per + c] = dot(grad_m[c], right_m[c])
    scatter(5, from_prod(5, per))

    arrived(4)
    to_stage(4, stage_b)
    for i in range(rows):
        grad = take(stage_b, i)
        gproj[2 * ch:3 * ch, i * res:(i + 1) * res] = (grad * fac_b[i]).astype(BF16)
        gproj[3 * ch:4 * ch, i * res:(i + 1) * res] = (grad * fac_gb[i]).astype(BF16)
    arrived(5)
    to_stage(5, stage_a)
    for i in range(rows):
        grad = take(stage_a, i)
        gproj[:ch, i * res:(i + 1) * res] = (grad * fac_a[i]).astype(BF16)
        gproj[ch:2 * ch, i * res:(i + 1) * res] = (grad * fac_ga[i]).astype(BF16)

    in_part = dot_nt(gproj[...], normed[...])
    part[...] = jnp.concatenate([in_part, out_part], axis=0).reshape(part.shape)

    def wsend(s, carry):
        peer = lax.rem(me + s, n_dap)
        pltpu.make_async_remote_copy(
            src_ref=part.at[peer], dst_ref=recv1.at[me],
            send_sem=wsend_sem.at[0], recv_sem=wrecv_sem.at[0],
            device_id={"dap": peer}, device_id_type=MESH,
        ).start()
        return carry

    lax.fori_loop(1, n_dap, wsend, 0)
    pltpu.make_async_copy(part.at[me], recv1.at[me], wrecv_sem.at[0]).start()

    def pair_out(i):
        grad = dot(win, gproj[:, i * res:(i + 1) * res]) * gin
        grad_pair = norm_back(grad, xhat[i], rstd_in[i]).astype(BF16)
        out_ref[i] = dot_nt(ident, grad_pair).astype(BF16)

    for i in range(rows // 2):
        pair_out(i)

    pltpu.make_async_copy(recv1, recv1, wrecv_sem.at[0]).wait()
    sum1[...] = jnp.sum(recv1[...], axis=0)

    def wexchange(s, carry):
        pltpu.make_async_remote_copy(
            src_ref=sum1, dst_ref=recv2.at[my_dp],
            send_sem=wsend_sem.at[1], recv_sem=wrecv_sem.at[1],
            device_id={"dp": lax.rem(my_dp + s, n_dp)}, device_id_type=MESH,
        ).start()
        return carry

    lax.fori_loop(1, n_dp, wexchange, 0)
    pltpu.make_async_copy(sum1, recv2.at[my_dp], wrecv_sem.at[1]).start()
    for i in range(rows // 2, rows * 3 // 4):
        pair_out(i)
    pltpu.make_async_copy(recv2, recv2, wrecv_sem.at[1]).wait()
    sum2[...] = jnp.sum(recv2[...], axis=0) * (1.0 / math.sqrt(n_dp * res * res))

    def wgather(s, carry):
        pltpu.make_async_remote_copy(
            src_ref=sum2, dst_ref=recv3.at[me],
            send_sem=wsend_sem.at[2], recv_sem=wrecv_sem.at[2],
            device_id={"dap": lax.rem(me + s, n_dap)}, device_id_type=MESH,
        ).start()
        return carry

    lax.fori_loop(1, n_dap, wgather, 0)
    pltpu.make_async_copy(sum2, recv3.at[me], wrecv_sem.at[2]).start()
    for i in range(rows * 3 // 4, rows):
        pair_out(i)
    pltpu.make_async_copy(recv3, recv3, wrecv_sem.at[2]).wait()
    total = recv3[...].reshape(6 * ch, ch)
    for block in range(5):
        inw_ref[:, block * ch:(block + 1) * ch] = total[block * ch:(block + 1) * ch].T
    outw_ref[...] = total[5 * ch:]

    for index in range(6):
        gone = send.at[index, pl.ds(0, n_dap - 1)]
        pltpu.make_async_copy(gone, gone, send_sem.at[index]).wait()
    gone = part.at[pl.ds(0, n_dap - 1)]
    pltpu.make_async_copy(gone, gone, wsend_sem.at[0]).wait()
    gone = recv2.at[pl.ds(0, n_dp - 1)]
    pltpu.make_async_copy(gone, gone, wsend_sem.at[1]).wait()
    gone = recv3.at[pl.ds(0, n_dap - 1)]
    pltpu.make_async_copy(gone, gone, wsend_sem.at[2]).wait()


def solution(mesh):
    n_dp, n_dap = mesh.shape["dp"], mesh.shape["dap"]

    def shards(pair_act, cotangent, residue_mask, in_gain, out_gain, in_weight, out_weight):
        _, rows, res, ch = pair_act.shape
        blk = ch // n_dap * rows
        per = ch // n_dap
        cells = rows * res
        wrows = 6 * ch // n_dap
        vmem = pl.BlockSpec(memory_space=pltpu.VMEM)
        out = pl.pallas_call(
            functools.partial(kernel, (n_dp, n_dap, rows, res, ch)),
            out_shape=(
                jax.ShapeDtypeStruct((rows, res, ch), BF16),
                jax.ShapeDtypeStruct((ch, 5 * ch), F32),
                jax.ShapeDtypeStruct((ch, ch), F32),
            ),
            in_specs=[vmem] * 7,
            out_specs=(vmem,) * 3,
            scratch_shapes=[
                pltpu.VMEM((6, n_dap, blk, res), BF16),
                pltpu.VMEM((6, n_dap, blk, res), BF16),
                pltpu.VMEM((ch * rows * res // LANES, LANES), F32),
                pltpu.VMEM((ch * rows * res // LANES, LANES), F32),
                pltpu.VMEM((per, res, res), BF16),
                pltpu.VMEM((per, res, res), BF16),
                pltpu.VMEM((per, res, res), BF16),
                pltpu.VMEM((2 * per, res, res), F32),
                pltpu.VMEM((rows, ch, res), F32),
                pltpu.VMEM((rows, 1, res), F32),
                pltpu.VMEM((ch, cells), BF16),
                pltpu.VMEM((rows, ch, res), F32),
                pltpu.VMEM((rows, ch, res), F32),
                pltpu.VMEM((rows, ch, res), F32),
                pltpu.VMEM((rows, ch, res), F32),
                pltpu.VMEM((rows, ch, res), F32),
                pltpu.VMEM((ch, cells), BF16),
                pltpu.VMEM((rows, ch, res), F32),
                pltpu.VMEM((ch, cells), BF16),
                pltpu.VMEM((5 * ch, cells), BF16),
                pltpu.VMEM((n_dap, wrows, ch), F32),
                pltpu.VMEM((n_dap, wrows, ch), F32),
                pltpu.VMEM((wrows, ch), F32),
                pltpu.VMEM((n_dp, wrows, ch), F32),
                pltpu.VMEM((wrows, ch), F32),
                pltpu.VMEM((n_dap, wrows, ch), F32),
                pltpu.SemaphoreType.DMA((6,)),
                pltpu.SemaphoreType.DMA((6,)),
                pltpu.SemaphoreType.DMA((3,)),
                pltpu.SemaphoreType.DMA((3,)),
            ],
            compiler_params=pltpu.CompilerParams(
                collective_id=0, has_side_effects=True, vmem_limit_bytes=56 * 2**20
            ),
            cost_estimate=pl.CostEstimate(
                flops=2 * 10**9, bytes_accessed=3 * 2**20, transcendentals=10**6
            ),
            name="triangle_backward",
        )(
            pair_act[0], cotangent[0], residue_mask,
            in_gain[None], out_gain[None], in_weight, out_weight,
        )
        return out[0][None], out[1], out[2]

    placed = (
        P("dp", "dap", None, None),
        P("dp", "dap", None, None),
        P("dp", None),
        P(),
        P(),
        P(),
        P(),
    )
    return jax.shard_map(
        shards,
        mesh=mesh,
        in_specs=placed,
        out_specs=(P("dp", "dap", None, None), P(), P()),
        check_vma=False,
    )
```
